32 devices in a mesh: row: 8 (over z, y), col: 4 (over x, core).
Axes of the slice: x: 2, y: 2, z: 4, core: 2. Of those that a mesh axis runs over, the one named last changes fastest.
Arguments:
- counts: int32 [1024, 262144], P('row', 'col'), may hold values from 0 to 7, as said below
- row_total: float32 [1024], P('row'), may hold values from 1 to 3670016, as said below
- col_total: float32 [262144], P('col'), may hold values from 1 to 3670528, as said below
- grand_total: float32 [1], replicated, as said below
- sketch: float32 [262144, 96], P(('col', 'row')), may hold values from -0.00036621094 to 0.00036621094
Outputs:
- column_factors: float32 [262144, 96], P(('col', 'row'))
- gram_factor: float32 [96, 96], replicated
The draws below stay inside these ranges and needn't reach their ends.
Inputs may be any that keep to these rules, and one draw needn't show every extreme that they name: About half of the counts are zero. `row_total`: each row's total is its counts' sum times a factor between 1 and 2. `col_total`: each item's total is its counts' sum over the slab plus one, times 262144 / 1024, times a factor between 1 and 2. `grand_total`: the grand total is the sum of col_total times a factor between 1 and 1.25.
All inputs are finite; a program needn't handle non-finite values.
Results may differ from the reference program's by a relative error of at most 0.0003.
Values sent between devices are 32-bit elements; how exact they have to be, the bound alone decides.
A program may use at most 128 MiB of HBM per device.

```python
import math
import jax
import jax.numpy as jnp
from jax import lax

C = 262144
K = 96
ROWS = 1024


def shared_counts(key):
    drawn = jax.random.randint(jax.random.fold_in(key, 101), (ROWS, C), -6, 8)
    return jnp.maximum(drawn, 0).astype(jnp.int32)


def column_marginal(key):
    slab_sums = jnp.sum(shared_counts(key), axis=0).astype(jnp.float32) + 1.0
    factor = jax.random.uniform(jax.random.fold_in(key, 202), (C,), jnp.float32, 1.0, 2.0)
    return slab_sums * float(C // ROWS) * factor


def draw_counts(key, part):
    return shared_counts(key)


def draw_row_total(key, part):
    row_sums = jnp.sum(shared_counts(key), axis=1).astype(jnp.float32)
    factor = jax.random.uniform(jax.random.fold_in(key, 303), (ROWS,), jnp.float32, 1.0, 2.0)
    return jnp.maximum(row_sums, 1.0) * factor


def draw_col_total(key, part):
    return column_marginal(key)


def draw_grand_total(key, part):
    whole = jnp.sum(column_marginal(key))
    factor = jax.random.uniform(jax.random.fold_in(key, 404), (1,), jnp.float32, 1.0, 1.25)
    return whole * factor


def block_scale(rng, shape, split, low, largest):
    loudness = 1.0
    for axis_at, blocks in split:
        heights = jax.random.uniform(jax.random.fold_in(jax.random.fold_in(rng, 6), axis_at), (blocks,), jnp.float32, low / len(split), largest / len(split))
        loudness = loudness * jnp.repeat(jnp.exp(heights), shape[axis_at] // blocks).reshape((-1,) + (1,) * (len(shape) - 1 - axis_at))
    return loudness


def normal_values(rng, dims, deviation, limit, pieces=(), kind=jnp.bfloat16):
    values = jax.random.normal(rng, dims, jnp.float32) * deviation
    if len(pieces) > 0:
        values = block_scale(rng, dims, pieces, -0.22, 0.18) * values
    return jnp.clip(values, min=-limit, max=limit).astype(kind)


def setup_inputs(seed: int = 0) -> dict:
    seeds = jax.random.split(jax.random.key(seed), 6)
    return {
        "counts": draw_counts(jax.random.fold_in(seeds[5], 71), 0),
        "row_total": draw_row_total(jax.random.fold_in(seeds[5], 71), 0),
        "col_total": draw_col_total(jax.random.fold_in(seeds[5], 71), 0),
        "grand_total": draw_grand_total(jax.random.fold_in(seeds[5], 71), 0),
        "sketch": normal_values(seeds[4], (C, K), (C * ROWS) ** -0.5, 0.00036621094, ((0, 32),), jnp.float32),
    }


def ppmi_block(counts_block, row_log, col_block):
    counts_float = counts_block.astype(jnp.float32)
    pmi = jnp.log(jnp.maximum(counts_float, 1.0)) + row_log[:, None] - jnp.log(col_block)[None, :]
    return jnp.where(counts_block > 0, jnp.maximum(pmi, 0.0), 0.0)

def reference(counts, row_total, col_total, grand_total, sketch):
    block_width = math.gcd(C, 8192)
    block_count = C // block_width
    row_log = jnp.log(grand_total[0]) - jnp.log(row_total)
    blocks = jnp.arange(block_count, dtype=jnp.int32)

    def tile_of(block):
        offset = (block * block_width).astype(jnp.int32)
        counts_block = lax.dynamic_slice_in_dim(counts, offset, block_width, 1)
        col_block = lax.dynamic_slice_in_dim(col_total, offset, block_width, 0)
        return ppmi_block(counts_block, row_log, col_block)

    def add_block(running, block):
        offset = (block * block_width).astype(jnp.int32)
        sketch_block = lax.dynamic_slice_in_dim(sketch, offset, block_width, 0)
        return (running + jnp.dot(tile_of(block).astype(jnp.float32), sketch_block.astype(jnp.float32), precision=lax.Precision.HIGHEST, preferred_element_type=jnp.float32), None)
    image, _ = lax.scan(add_block, jnp.zeros((ROWS, K), jnp.float32), blocks)
    gram_matrix = jnp.dot(image.T.astype(jnp.float32), image.astype(jnp.float32), precision=lax.Precision.HIGHEST, preferred_element_type=jnp.float32)
    factor = jnp.linalg.cholesky(gram_matrix)
    basis = jax.scipy.linalg.solve_triangular(factor, image.T, lower=True).T

    def column_block(block):
        return jnp.dot(tile_of(block).T.astype(jnp.float32), basis.astype(jnp.float32), precision=lax.Precision.HIGHEST, preferred_element_type=jnp.float32)
    column_factors = lax.map(column_block, blocks).reshape(C, K)
    return (column_factors, factor)
```

```python
import functools

import jax
import jax.numpy as jnp
from jax import lax
from jax.experimental import pallas as pl
from jax.experimental.pallas import tpu as pltpu
from jax.sharding import PartitionSpec as P

MESH = pl.DeviceIdType.MESH
VMEM_BYTES = 56 * 2**20
F32, BF16 = jnp.float32, jnp.bfloat16


def ring_place(row, n):
    odd = lax.rem(row, 2)
    up = lax.div(row, 2)
    return (1 - odd) * up + odd * (n - 1 - up)


def ring_row(place, n):
    back = lax.div(place, n // 2)
    return (1 - back) * 2 * place + back * (2 * (n - 1 - place) + 1)


def neighbours(n):
    me = ring_place(lax.axis_index("row"), n)
    after = ring_row(lax.rem(me + 1, n), n)
    before = ring_row(lax.rem(me + n - 1, n), n)
    return me, after, before


def meet(after, before):
    barrier = pltpu.get_barrier_semaphore()
    for row in (after, before):
        pl.semaphore_signal(
            barrier, inc=1, device_id=(row, lax.axis_index("col")), device_id_type=MESH
        )
    pl.semaphore_wait(barrier, 2)


def split(x):
    high = x.astype(BF16)
    return high, (x - high.astype(F32)).astype(BF16)


def ppmi_parts(counts, row_log, col_total):
    pmi = jnp.log(jnp.maximum(counts.astype(F32), 1.0)) + row_log - jnp.log(col_total)
    ppmi = jnp.where(counts > 0, jnp.maximum(pmi, 0.0), 0.0)
    return jnp.concatenate(split(ppmi), axis=0)


def tile_width(half):
    width = 1024
    while half % width:
        width //= 2
    return width


def columns_of(place, half, width, n):
    return pl.multiple_of(ring_row(place, n) * (2 * width) + half * width, 128)


def counts_copy(counts_ref, held, sem, item, start, width):
    slot = lax.rem(item, 2)
    return pltpu.make_async_copy(
        counts_ref.at[:, pl.ds(start, width)], held.at[slot], sem.at[slot]
    )


def gather_kernel(
    n, counts_ref, row_log_ref, col_ref, sketch_ref, image_ref,
    buf, held, total, send_sem, recv_sem, counts_sem, own_sem,
):
    width = buf.shape[3]
    rank = buf.shape[2]
    rows = row_log_ref.shape[0]
    tile = tile_width(width)
    me, after, before = neighbours(n)
    col = lax.axis_index("col")

    def where_of(item):
        extra = lax.max(item - 2, 0)
        far = lax.min(lax.div(item, 2), 1)
        way = far * lax.rem(extra, 2)
        slot = (1 - far) * item + far * (2 + lax.div(extra, 2))
        distance = lax.div(slot, 2)
        odd = lax.rem(slot, 2)
        half = (1 - way) * odd + way * (1 - odd)
        place = lax.rem(me + n + (2 * way - 1) * distance, n)
        return way, slot, columns_of(place, half, width, n)

    def send(way, slot):
        return pltpu.make_async_remote_copy(
            src_ref=buf.at[way, slot],
            dst_ref=buf.at[way, slot + 2],
            send_sem=send_sem.at[way, slot],
            recv_sem=recv_sem.at[way, slot],
            device_id=((1 - way) * after + way * before, col),
            device_id_type=MESH,
        )

    def counts_of(item):
        return counts_copy(counts_ref, held, counts_sem, item, where_of(item)[2], width)

    own = [
        pltpu.make_async_copy(
            sketch_ref.at[:, pl.ds((slot if way == 0 else 1 - slot) * width, width)],
            buf.at[way, slot],
            own_sem.at[way, slot],
        )
        for slot in range(2)
        for way in range(2)
    ]
    for copy in own:
        copy.start()
    counts_of(0).start()
    meet(after, before)
    for at, copy in enumerate(own):
        copy.wait()
        send(at % 2, at // 2).start()
    total[...] = jnp.zeros_like(total)

    def step(item, carry):
        way, slot, start = where_of(item)

        @pl.when(item + 1 < 2 * n)
        def _():
            counts_of(item + 1).start()

        @pl.when(item >= 2)
        def _():
            send(way, slot - 2).wait_recv()

            @pl.when(slot <= n - 2)
            def _():
                send(way, slot).start()

        counts_of(item).wait()
        at = lax.rem(item, 2)

        def piece(t, carry):
            here = pl.ds(pl.multiple_of(t * tile, tile), tile)
            parts = ppmi_parts(
                held[at, :, here],
                row_log_ref[...],
                col_ref[:, pl.ds(pl.multiple_of(start + t * tile, 128), tile)],
            )
            high, low = split(buf[way, slot, :, here])
            gap = jnp.zeros((128 - rank % 128, tile), BF16)
            test = jnp.concatenate([high, gap, low, gap], axis=0)
            total[...] += lax.dot_general(
                parts, test, (((1,), (1,)), ((), ())), preferred_element_type=F32
            )
            return carry

        lax.fori_loop(0, width // tile, piece, 0)
        return carry

    lax.fori_loop(0, 2 * n, step, 0)
    wide = total.shape[1] // 2
    both = total[:rows, :] + total[rows:, :]
    image_ref[...] = (both[:, :wide] + both[:, wide:])[:, :rank]

    def sent(slot, carry):
        send(0, slot).wait_send()
        send(1, slot).wait_send()
        return carry

    lax.fori_loop(0, n - 1, sent, 0)


def scatter_kernel(
    n, counts_ref, row_log_ref, col_ref, image_ref, out_ref,
    buf, held, left, send_sem, recv_sem, counts_sem,
):
    width = buf.shape[3]
    rank = buf.shape[2]
    tile = tile_width(width)
    me, after, before = neighbours(n)
    col = lax.axis_index("col")

    def where_of(item):
        way = lax.rem(item, 2)
        own = lax.div(item, 2 * n - 2)
        slot = (1 - own) * (n - lax.div(item, 2)) + own * (n + 1)
        distance = (1 - own) * lax.div(slot, 2)
        odd = lax.rem(slot, 2)
        half = (1 - own) * ((1 - way) * odd + way * (1 - odd)) + own * way
        place = lax.rem(me + n + (1 - 2 * way) * distance, n)
        return way, slot, columns_of(place, half, width, n)

    def send(way, slot):
        return pltpu.make_async_remote_copy(
            src_ref=buf.at[way, slot + 2],
            dst_ref=buf.at[way, slot],
            send_sem=send_sem.at[way, slot],
            recv_sem=recv_sem.at[way, slot],
            device_id=((1 - way) * after + way * before, col),
            device_id_type=MESH,
        )

    def counts_of(item):
        return counts_copy(counts_ref, held, counts_sem, item, where_of(item)[2], width)

    counts_of(0).start()
    high, low = split(image_ref[...])
    left[...] = jnp.concatenate(
        [jnp.concatenate([high, high], axis=1), jnp.concatenate([low, low], axis=1)], axis=0
    )
    meet(after, before)

    def step(item, carry):
        way, slot, start = where_of(item)
        arrives = slot <= n - 2

        @pl.when(item + 1 < 2 * n)
        def _():
            counts_of(item + 1).start()

        counts_of(item).wait()

        @pl.when(arrives)
        def _():
            send(way, slot).wait_recv()

        at = lax.rem(item, 2)

        def piece(t, carry):
            here = pl.ds(pl.multiple_of(t * tile, tile), tile)
            parts = ppmi_parts(
                held[at, :, here],
                row_log_ref[...],
                col_ref[:, pl.ds(pl.multiple_of(start + t * tile, 128), tile)],
            )
            product = jnp.dot(left[...], parts, preferred_element_type=F32)
            product = product[:rank] + product[rank:]

            @pl.when(arrives)
            def _():
                buf[way, slot, :, here] = buf[way, slot, :, here] + product

            @pl.when(jnp.logical_not(arrives))
            def _():
                buf[way, slot, :, here] = product

            return carry

        lax.fori_loop(0, width // tile, piece, 0)

        @pl.when(slot <= n)
        def _():
            send(way, slot - 2).start()

        return carry

    lax.fori_loop(0, 2 * n, step, 0)
    for slot in (1, 0):
        for way in range(2):
            send(way, slot).wait_recv()
    for half in range(2):
        def add(t, carry, half=half):
            here = pl.ds(pl.multiple_of(t * tile, tile), tile)
            there = pl.ds(pl.multiple_of(half * width + t * tile, tile), tile)
            out_ref[:, there] = (
                buf[half, n + 1, :, here] + buf[0, half, :, here] + buf[1, 1 - half, :, here]
            )
            return carry

        lax.fori_loop(0, width // tile, add, 0)

    def sent(slot, carry):
        send(0, slot).wait_send()
        send(1, slot).wait_send()
        return carry

    lax.fori_loop(0, n - 1, sent, 0)


def per_device(n, counts, row_total, col_total, grand_total, sketch):
    rows, columns = counts.shape
    shard, rank = sketch.shape
    width = shard // 2
    row_log = (jnp.log(grand_total[0]) - jnp.log(row_total))[:, None]
    col_row = col_total[None, :]
    vmem, anywhere = pl.BlockSpec(memory_space=pltpu.VMEM), pl.BlockSpec(memory_space=pl.ANY)
    cost = pl.CostEstimate(
        flops=8 * rows * columns * rank, bytes_accessed=4 * rows * columns, transcendentals=rows * columns
    )
    dma = pltpu.SemaphoreType.DMA
    padded = (rank + 127) // 128 * 128

    partial_image = pl.pallas_call(
        functools.partial(gather_kernel, n),
        out_shape=jax.ShapeDtypeStruct((rows, rank), F32),
        in_specs=[anywhere, vmem, vmem, anywhere],
        out_specs=vmem,
        scratch_shapes=[
            pltpu.VMEM((2, n + 1, rank, width), F32),
            pltpu.VMEM((2, rows, width), jnp.int32),
            pltpu.VMEM((2 * rows, 2 * padded), F32),
            dma((2, n - 1)),
            dma((2, n - 1)),
            dma((2,)),
            dma((2, 2)),
        ],
        compiler_params=pltpu.CompilerParams(
            collective_id=0, has_side_effects=True, vmem_limit_bytes=VMEM_BYTES
        ),
        cost_estimate=cost,
        name="gather_image",
    )(counts, row_log, col_row, sketch.T)

    image = lax.psum(partial_image, "col")
    gram_local = jnp.dot(
        image.T, image, precision=lax.Precision.HIGHEST, preferred_element_type=F32
    )
    gram_matrix = lax.psum(gram_local, "row")
    factor = jnp.linalg.cholesky(gram_matrix)

    summed = pl.pallas_call(
        functools.partial(scatter_kernel, n),
        out_shape=jax.ShapeDtypeStruct((rank, shard), F32),
        in_specs=[anywhere, vmem, vmem, vmem],
        out_specs=vmem,
        scratch_shapes=[
            pltpu.VMEM((2, n + 2, rank, width), F32),
            pltpu.VMEM((2, rows, width), jnp.int32),
            pltpu.VMEM((2 * rank, 2 * rows), BF16),
            dma((2, n - 1)),
            dma((2, n - 1)),
            dma((2,)),
        ],
        compiler_params=pltpu.CompilerParams(
            collective_id=1, has_side_effects=True, vmem_limit_bytes=VMEM_BYTES
        ),
        cost_estimate=cost,
        name="scatter_columns",
    )(counts, row_log, col_row, image.T)
    column_factors = jax.scipy.linalg.solve_triangular(factor, summed, lower=True).T
    return (column_factors, factor)


def solution(mesh):
    return jax.shard_map(
        functools.partial(per_device, mesh.shape["row"]),
        mesh=mesh,
        in_specs=(P("row", "col"), P("row"), P("col"), P(), P(("col", "row"), None)),
        out_specs=(P(("col", "row"), None), P()),
        check_vma=False,
    )
```

```python
import functools

import jax
import jax.numpy as jnp
from jax import lax
from jax.experimental import pallas as pl
from jax.experimental.pallas import tpu as pltpu
from jax.sharding import PartitionSpec as P

MESH = pl.DeviceIdType.MESH
VMEM_BYTES = 56 * 2**20
F32, BF16 = jnp.float32, jnp.bfloat16


def ring_place(row, n):
    odd = lax.rem(row, 2)
    up = lax.div(row, 2)
    return (1 - odd) * up + odd * (n - 1 - up)


def ring_row(place, n):
    back = lax.div(place, n // 2)
    return (1 - back) * 2 * place + back * (2 * (n - 1 - place) + 1)


def neighbours(n):
    me = ring_place(lax.axis_index("row"), n)
    after = ring_row(lax.rem(me + 1, n), n)
    before = ring_row(lax.rem(me + n - 1, n), n)
    return me, after, before


def meet(n, m):
    row, col = lax.axis_index("row"), lax.axis_index("col")
    barrier = pltpu.get_barrier_semaphore()
    for d in range(1, n):
        pl.semaphore_signal(
            barrier, inc=1, device_id=(lax.rem(row + d, n), col), device_id_type=MESH
        )
    for d in range(1, m):
        pl.semaphore_signal(
            barrier, inc=1, device_id=(row, lax.rem(col + d, m)), device_id_type=MESH
        )
    pl.semaphore_wait(barrier, n + m - 2)


def split(x):
    high = x.astype(BF16)
    return high, (x - high.astype(F32)).astype(BF16)


def ppmi_parts(counts, row_log, col_total):
    pmi = jnp.log(jnp.maximum(counts.astype(F32), 1.0)) + row_log - jnp.log(col_total)
    ppmi = jnp.where(counts > 0, jnp.maximum(pmi, 0.0), 0.0)
    return jnp.concatenate(split(ppmi), axis=0)


def tile_width(half):
    width = 1024
    while half % width:
        width //= 2
    return width


def columns_of(place, half, width, n):
    return pl.multiple_of(ring_row(place, n) * (2 * width) + half * width, 128)


def counts_copy(counts_ref, held, sem, item, start, width):
    slot = lax.rem(item, 2)
    return pltpu.make_async_copy(
        counts_ref.at[:, pl.ds(start, width)], held.at[slot], sem.at[slot]
    )


def twice(x):
    high, low = split(x)
    return jnp.concatenate(
        [jnp.concatenate([high, high], axis=1), jnp.concatenate([low, low], axis=1)], axis=0
    )


def eliminate(work, k):
    rank, wide = work.shape
    lanes = lax.broadcasted_iota(jnp.int32, (1, wide // 2), 1)
    rows = lax.broadcasted_iota(jnp.int32, (rank, 1), 0)
    now = work[...]
    row = work[pl.ds(k, 1), :]
    column = jnp.sum(jnp.where(lanes == k, now[:, : wide // 2], 0.0), axis=1, keepdims=True)
    pivot = jnp.sum(jnp.where(lanes == k, row[:, : wide // 2], 0.0), axis=1, keepdims=True)
    root = jnp.sqrt(pivot)
    row = row / root
    rest = now - jnp.where(rows > k, column / root, 0.0) * row
    work[...] = jnp.where(rows == k, row, rest)


def round_kernel(
    n, m, counts_ref, row_log_ref, col_ref, sketch_ref, out_ref, upper_ref,
    buf, held, total, images, grams, left, work,
    send_g, recv_g, send_s, recv_s, counts_sem, own_sem,
    send_i, recv_i, send_m, recv_m, ready,
):
    width = buf.shape[3]
    rank = buf.shape[2]
    rows = row_log_ref.shape[0]
    tile = tile_width(width)
    me, after, before = neighbours(n)
    my_row, col = lax.axis_index("row"), lax.axis_index("col")

    def target(way):
        return ((1 - way) * after + way * before, col)

    def gather_item(item):
        extra = lax.max(item - 2, 0)
        far = lax.min(lax.div(item, 2), 1)
        way = far * lax.rem(extra, 2)
        slot = (1 - far) * item + far * (2 + lax.div(extra, 2))
        distance = lax.div(slot, 2)
        odd = lax.rem(slot, 2)
        half = (1 - way) * odd + way * (1 - odd)
        place = lax.rem(me + n + (2 * way - 1) * distance, n)
        return way, slot, columns_of(place, half, width, n)

    def scatter_item(item):
        way = lax.rem(item, 2)
        own = lax.div(item, 2 * n - 2)
        slot = (1 - own) * (n - lax.div(item, 2)) + own * (n + 1)
        distance = (1 - own) * lax.div(slot, 2)
        odd = lax.rem(slot, 2)
        half = (1 - own) * ((1 - way) * odd + way * (1 - odd)) + own * way
        place = lax.rem(me + n + (1 - 2 * way) * distance, n)
        return way, slot, columns_of(place, half, width, n)

    def send_sketch(way, slot):
        return pltpu.make_async_remote_copy(
            src_ref=buf.at[way, slot],
            dst_ref=buf.at[way, slot + 2],
            send_sem=send_g.at[way, slot],
            recv_sem=recv_g.at[way, slot],
            device_id=target(way),
            device_id_type=MESH,
        )

    def send_sums(way, slot):
        return pltpu.make_async_remote_copy(
            src_ref=buf.at[way, slot + 2],
            dst_ref=buf.at[way, slot],
            send_sem=send_s.at[way, slot],
            recv_sem=recv_s.at[way, slot],
            device_id=target(way),
            device_id_type=MESH,
        )

    def gather_counts(item):
        return counts_copy(counts_ref, held, counts_sem, item, gather_item(item)[2], width)

    def scatter_counts(item):
        return counts_copy(counts_ref, held, counts_sem, item, scatter_item(item)[2], width)

    def ppmi_at(item, start, t):
        return ppmi_parts(
            held[lax.rem(item, 2), :, pl.ds(pl.multiple_of(t * tile, tile), tile)],
            row_log_ref[...],
            col_ref[:, pl.ds(pl.multiple_of(start + t * tile, 128), tile)],
        )

    own = [
        pltpu.make_async_copy(
            sketch_ref.at[:, pl.ds((slot if way == 0 else 1 - slot) * width, width)],
            buf.at[way, slot],
            own_sem.at[way, slot],
        )
        for slot in range(2)
        for way in range(2)
    ]
    for copy in own:
        copy.start()
    gather_counts(0).start()
    meet(n, m)
    for at, copy in enumerate(own):
        copy.wait()
        send_sketch(at % 2, at // 2).start()
    total[...] = jnp.zeros_like(total)

    def gather_step(item, carry):
        way, slot, start = gather_item(item)

        @pl.when(item + 1 < 2 * n)
        def _():
            gather_counts(item + 1).start()

        @pl.when(item >= 2)
        def _():
            send_sketch(way, slot - 2).wait_recv()

            @pl.when(slot <= n - 2)
            def _():
                send_sketch(way, slot).start()

        gather_counts(item).wait()

        def piece(t, carry):
            here = pl.ds(pl.multiple_of(t * tile, tile), tile)
            test = jnp.concatenate(split(buf[way, slot, :, here]), axis=0)
            total[...] += lax.dot_general(
                test, ppmi_at(item, start, t), (((1,), (1,)), ((), ())),
                preferred_element_type=F32,
            )
            return carry

        lax.fori_loop(0, width // tile, piece, 0)
        return carry

    lax.fori_loop(0, 2 * n, gather_step, 0)
    scatter_counts(0).start()

    both = total[:rank, :] + total[rank:, :]
    images[col] = both[:, :rows] + both[:, rows:]

    def image_copy(sender, receiver):
        return pltpu.make_async_remote_copy(
            src_ref=images.at[sender],
            dst_ref=images.at[sender],
            send_sem=send_i.at[receiver],
            recv_sem=recv_i.at[sender],
            device_id=(my_row, receiver),
            device_id_type=MESH,
        )

    others = [lax.rem(col + d, m) for d in range(1, m)]
    for other in others:
        image_copy(col, other).start()

    def sketch_sent(slot, carry):
        send_sketch(0, slot).wait_send()
        send_sketch(1, slot).wait_send()
        return carry

    lax.fori_loop(0, n - 1, sketch_sent, 0)
    for way in range(2):
        pl.semaphore_signal(ready, inc=1, device_id=target(way), device_id_type=MESH)
    for other in others:
        image_copy(other, col).wait_recv()
    image = images[0]
    for c in range(1, m):
        image = image + images[c]
    left[...] = twice(image)

    grams[my_row] = lax.dot_general(
        image, image, (((1,), (1,)), ((), ())),
        precision=lax.Precision.HIGHEST, preferred_element_type=F32,
    )

    def gram_copy(sender, receiver):
        return pltpu.make_async_remote_copy(
            src_ref=grams.at[sender],
            dst_ref=grams.at[sender],
            send_sem=send_m.at[receiver],
            recv_sem=recv_m.at[sender],
            device_id=(receiver, col),
            device_id_type=MESH,
        )

    peers = [lax.rem(my_row + d, n) for d in range(1, n)]
    for peer in peers:
        gram_copy(my_row, peer).start()
    pl.semaphore_wait(ready, 2)

    pieces = min(8, n)
    first = n // 2
    wide = work.shape[1] // 2

    def scatter_step(item, carry):
        way, slot, start = scatter_item(item)
        arrives = slot <= n - 2

        @pl.when(item + 1 < 2 * n)
        def _():
            scatter_counts(item + 1).start()

        scatter_counts(item).wait()

        @pl.when(arrives)
        def _():
            send_sums(way, slot).wait_recv()

        def piece(t, carry):
            here = pl.ds(pl.multiple_of(t * tile, tile), tile)
            product = jnp.dot(left[...], ppmi_at(item, start, t), preferred_element_type=F32)
            product = product[:rank] + product[rank:]

            @pl.when(arrives)
            def _():
                buf[way, slot, :, here] = buf[way, slot, :, here] + product

            @pl.when(jnp.logical_not(arrives))
            def _():
                buf[way, slot, :, here] = product

            return carry

        lax.fori_loop(0, width // tile, piece, 0)

        @pl.when(slot <= n)
        def _():
            send_sums(way, slot - 2).start()

        @pl.when(item == first)
        def _():
            for peer in peers:
                gram_copy(peer, my_row).wait_recv()
            gram = grams[0]
            for r in range(1, n):
                gram = gram + grams[r]
            work[...] = jnp.zeros_like(work)
            work[:, :rank] = gram
            shape = (rank, wide)
            same = lax.broadcasted_iota(jnp.int32, shape, 0) == lax.broadcasted_iota(
                jnp.int32, shape, 1
            )
            work[:, wide:] = jnp.where(same, 1.0, 0.0)

        @pl.when(jnp.logical_and(item >= first, item < first + pieces))
        def _():
            steps = rank // pieces

            def turn(k, carry):
                eliminate(work, (item - first) * steps + k)
                return carry

            lax.fori_loop(0, steps, turn, 0)

        return carry

    lax.fori_loop(0, 2 * n, scatter_step, 0)
    above = lax.broadcasted_iota(jnp.int32, (rank, wide), 0) <= lax.broadcasted_iota(
        jnp.int32, (rank, wide), 1
    )
    upper_ref[...] = jnp.where(above, work[:, :wide], 0.0)[:, :rank]
    inverse = twice(work[:, wide:])
    for slot in (1, 0):
        for way in range(2):
            send_sums(way, slot).wait_recv()
    for half in range(2):
        def finish(t, carry, half=half):
            here = pl.ds(pl.multiple_of(t * tile, tile), tile)
            there = pl.ds(pl.multiple_of(half * width + t * tile, tile), tile)
            high, low = split(
                buf[half, n + 1, :, here] + buf[0, half, :, here] + buf[1, 1 - half, :, here]
            )
            gap = jnp.zeros((wide - rank, tile), BF16)
            sums = jnp.concatenate([high, gap, low, gap], axis=0)
            product = jnp.dot(inverse, sums, preferred_element_type=F32)
            out_ref[:, there] = product[:rank] + product[rank:]
            return carry

        lax.fori_loop(0, width // tile, finish, 0)

    def sums_sent(slot, carry):
        send_sums(0, slot).wait_send()
        send_sums(1, slot).wait_send()
        return carry

    lax.fori_loop(0, n - 1, sums_sent, 0)
    for other in others:
        image_copy(col, other).wait_send()
    for peer in peers:
        gram_copy(my_row, peer).wait_send()


def per_device(n, m, counts, row_total, col_total, grand_total, sketch):
    rows, columns = counts.shape
    shard, rank = sketch.shape
    width = shard // 2
    row_log = (jnp.log(grand_total[0]) - jnp.log(row_total))[:, None]
    vmem, anywhere = pl.BlockSpec(memory_space=pltpu.VMEM), pl.BlockSpec(memory_space=pl.ANY)
    dma = pltpu.SemaphoreType.DMA
    padded = (rank + 127) // 128 * 128
    column_factors, upper = pl.pallas_call(
        functools.partial(round_kernel, n, m),
        out_shape=[
            jax.ShapeDtypeStruct((rank, shard), F32),
            jax.ShapeDtypeStruct((rank, rank), F32),
        ],
        in_specs=[anywhere, vmem, vmem, anywhere],
        out_specs=[vmem, vmem],
        scratch_shapes=[
            pltpu.VMEM((2, n + 2, rank, width), F32),
            pltpu.VMEM((2, rows, width), jnp.int32),
            pltpu.VMEM((2 * rank, 2 * rows), F32),
            pltpu.VMEM((m, rank, rows), F32),
            pltpu.VMEM((n, rank, rank), F32),
            pltpu.VMEM((2 * rank, 2 * rows), BF16),
            pltpu.VMEM((rank, 2 * padded), F32),
            dma((2, n - 1)),
            dma((2, n - 1)),
            dma((2, n - 1)),
            dma((2, n - 1)),
            dma((2,)),
            dma((2, 2)),
            dma((m,)),
            dma((m,)),
            dma((n,)),
            dma((n,)),
            pltpu.SemaphoreType.REGULAR,
        ],
        compiler_params=pltpu.CompilerParams(
            collective_id=0, has_side_effects=True, vmem_limit_bytes=VMEM_BYTES
        ),
        cost_estimate=pl.CostEstimate(
            flops=16 * rows * columns * rank,
            bytes_accessed=8 * rows * columns,
            transcendentals=2 * rows * columns,
        ),
        name="power_round",
    )(counts, row_log, col_total[None, :], sketch.T)
    return (column_factors.T, upper.T)


def solution(mesh):
    return jax.shard_map(
        functools.partial(per_device, mesh.shape["row"], mesh.shape["col"]),
        mesh=mesh,
        in_specs=(P("row", "col"), P("row"), P("col"), P(), P(("col", "row"), None)),
        out_specs=(P(("col", "row"), None), P()),
        check_vma=False,
    )
```

```python
import functools

import jax
import jax.numpy as jnp
from jax import lax
from jax.experimental import pallas as pl
from jax.experimental.pallas import tpu as pltpu
from jax.sharding import PartitionSpec as P

MESH = pl.DeviceIdType.MESH
VMEM_BYTES = 56 * 2**20
PARTS = 4
AHEAD = 3
F32, BF16 = jnp.float32, jnp.bfloat16


def ring_place(row, n):
    odd = lax.rem(row, 2)
    up = lax.div(row, 2)
    return (1 - odd) * up + odd * (n - 1 - up)


def ring_row(place, n):
    back = lax.div(place, n // 2)
    return (1 - back) * 2 * place + back * (2 * (n - 1 - place) + 1)


def neighbours(n):
    me = ring_place(lax.axis_index("row"), n)
    after = ring_row(lax.rem(me + 1, n), n)
    before = ring_row(lax.rem(me + n - 1, n), n)
    return me, after, before


def meet(n, m):
    row, col = lax.axis_index("row"), lax.axis_index("col")
    barrier = pltpu.get_barrier_semaphore()
    for d in range(1, n):
        pl.semaphore_signal(
            barrier, inc=1, device_id=(lax.rem(row + d, n), col), device_id_type=MESH
        )
    for d in range(1, m):
        pl.semaphore_signal(
            barrier, inc=1, device_id=(row, lax.rem(col + d, m)), device_id_type=MESH
        )
    pl.semaphore_wait(barrier, n + m - 2)


def split(x):
    high = x.astype(BF16)
    return high, (x - high.astype(F32)).astype(BF16)


def ppmi_parts(counts, row_log, col_total):
    pmi = jnp.log(jnp.maximum(counts.astype(F32), 1.0)) + row_log - jnp.log(col_total)
    ppmi = jnp.where(counts > 0, jnp.maximum(pmi, 0.0), 0.0)
    return jnp.concatenate(split(ppmi), axis=0)


def tile_width(half):
    width = 1024
    while half % width:
        width //= 2
    return width


def columns_of(place, half, part, width, n):
    start = ring_row(place, n) * (2 * PARTS * width) + (half * PARTS + part) * width
    return pl.multiple_of(start, 128)


def counts_copy(counts_ref, held, sem, item, start, width):
    slot = lax.rem(item, AHEAD + 1)
    return pltpu.make_async_copy(
        counts_ref.at[:, pl.ds(start, width)], held.at[slot], sem.at[slot]
    )


def twice(x):
    high, low = split(x)
    return jnp.concatenate(
        [jnp.concatenate([high, high], axis=1), jnp.concatenate([low, low], axis=1)], axis=0
    )


def eliminate(work, k):
    rank, wide = work.shape
    lanes = lax.broadcasted_iota(jnp.int32, (1, wide // 2), 1)
    rows = lax.broadcasted_iota(jnp.int32, (rank, 1), 0)
    now = work[...]
    row = work[pl.ds(k, 1), :]
    column = jnp.sum(jnp.where(lanes == k, now[:, : wide // 2], 0.0), axis=1, keepdims=True)
    pivot = jnp.sum(jnp.where(lanes == k, row[:, : wide // 2], 0.0), axis=1, keepdims=True)
    root = jnp.sqrt(pivot)
    row = row / root
    rest = now - jnp.where(rows > k, column / root, 0.0) * row
    work[...] = jnp.where(rows == k, row, rest)


def round_kernel(
    n, m, counts_ref, row_log_ref, col_ref, sketch_ref, out_ref, upper_ref,
    buf, held, total, images, grams, left, work,
    send_g, recv_g, send_s, recv_s, counts_sem, own_sem,
    send_i, recv_i, send_m, recv_m, ready,
):
    width = buf.shape[3]
    rank = buf.shape[2]
    rows = row_log_ref.shape[0]
    tile = tile_width(width)
    me, after, before = neighbours(n)
    my_row, col = lax.axis_index("row"), lax.axis_index("col")
    last = (n - 1) * PARTS
    items = 2 * n * PARTS

    def target(way):
        return ((1 - way) * after + way * before, col)

    def gather_item(item):
        extra = lax.max(item - 2 * PARTS, 0)
        far = lax.min(lax.div(item, 2 * PARTS), 1)
        way = far * lax.rem(extra, 2)
        spot = (1 - far) * item + far * (2 * PARTS + lax.div(extra, 2))
        slot, part = lax.div(spot, PARTS), lax.rem(spot, PARTS)
        distance = lax.div(slot, 2)
        odd = lax.rem(slot, 2)
        half = (1 - way) * odd + way * (1 - odd)
        place = lax.rem(me + n + (2 * way - 1) * distance, n)
        return way, spot, columns_of(place, half, part, width, n)

    def scatter_item(item):
        way = lax.rem(item, 2)
        count = lax.div(item, 2)
        own = lax.div(count, last)
        spot = (1 - own) * (last + 2 * PARTS - 1 - count) + own * (2 * PARTS + count)
        slot, part = lax.div(spot, PARTS), lax.rem(spot, PARTS)
        distance = (1 - own) * lax.div(slot, 2)
        odd = lax.rem(slot, 2)
        half = (1 - own) * ((1 - way) * odd + way * (1 - odd)) + own * way
        place = lax.rem(me + n + (1 - 2 * way) * distance, n)
        return way, spot, columns_of(place, half, part, width, n)

    def send_sketch(way, spot):
        return pltpu.make_async_remote_copy(
            src_ref=buf.at[way, spot],
            dst_ref=buf.at[way, spot + 2 * PARTS],
            send_sem=send_g.at[way, spot],
            recv_sem=recv_g.at[way, spot],
            device_id=target(way),
            device_id_type=MESH,
        )

    def send_sums(way, spot):
        return pltpu.make_async_remote_copy(
            src_ref=buf.at[way, spot + 2 * PARTS],
            dst_ref=buf.at[way, spot],
            send_sem=send_s.at[way, spot],
            recv_sem=recv_s.at[way, spot],
            device_id=target(way),
            device_id_type=MESH,
        )

    def gather_counts(item):
        return counts_copy(counts_ref, held, counts_sem, item, gather_item(item)[2], width)

    def scatter_counts(item):
        return counts_copy(counts_ref, held, counts_sem, item, scatter_item(item)[2], width)

    def ppmi_at(item, start, t):
        return ppmi_parts(
            held[lax.rem(item, AHEAD + 1), :, pl.ds(pl.multiple_of(t * tile, tile), tile)],
            row_log_ref[...],
            col_ref[:, pl.ds(pl.multiple_of(start + t * tile, 128), tile)],
        )

    own = [
        pltpu.make_async_copy(
            sketch_ref.at[:, pl.ds(((spot + way * PARTS) % (2 * PARTS)) * width, width)],
            buf.at[way, spot],
            own_sem.at[way, spot],
        )
        for spot in range(2 * PARTS)
        for way in range(2)
    ]
    for copy in own:
        copy.start()
    for item in range(AHEAD):
        gather_counts(item).start()
    meet(n, m)
    for at, copy in enumerate(own):
        copy.wait()
        send_sketch(at % 2, at // 2).start()
    total[...] = jnp.zeros_like(total)

    def gather_step(item, carry):
        way, spot, start = gather_item(item)

        @pl.when(item + AHEAD < items)
        def _():
            gather_counts(item + AHEAD).start()

        @pl.when(item >= 2 * PARTS)
        def _():
            send_sketch(way, spot - 2 * PARTS).wait_recv()

            @pl.when(spot < last)
            def _():
                send_sketch(way, spot).start()

        gather_counts(item).wait()

        def piece(t, carry):
            here = pl.ds(pl.multiple_of(t * tile, tile), tile)
            test = jnp.concatenate(split(buf[way, spot, :, here]), axis=0)
            total[...] += lax.dot_general(
                test, ppmi_at(item, start, t), (((1,), (1,)), ((), ())),
                preferred_element_type=F32,
            )
            return carry

        lax.fori_loop(0, width // tile, piece, 0)
        return carry

    lax.fori_loop(0, items, gather_step, 0)
    for item in range(AHEAD):
        scatter_counts(item).start()

    both = total[:rank, :] + total[rank:, :]
    images[col] = both[:, :rows] + both[:, rows:]

    def image_copy(sender, receiver):
        return pltpu.make_async_remote_copy(
            src_ref=images.at[sender],
            dst_ref=images.at[sender],
            send_sem=send_i.at[receiver],
            recv_sem=recv_i.at[sender],
            device_id=(my_row, receiver),
            device_id_type=MESH,
        )

    others = [lax.rem(col + d, m) for d in range(1, m)]
    for other in others:
        image_copy(col, other).start()

    def sketch_sent(spot, carry):
        send_sketch(0, spot).wait_send()
        send_sketch(1, spot).wait_send()
        return carry

    lax.fori_loop(0, last, sketch_sent, 0)
    for way in range(2):
        pl.semaphore_signal(ready, inc=1, device_id=target(way), device_id_type=MESH)
    for other in others:
        image_copy(other, col).wait_recv()
    image = images[0]
    for c in range(1, m):
        image = image + images[c]
    left[...] = twice(image)

    grams[my_row] = lax.dot_general(
        image, image, (((1,), (1,)), ((), ())),
        precision=lax.Precision.HIGHEST, preferred_element_type=F32,
    )

    def gram_copy(sender, receiver):
        return pltpu.make_async_remote_copy(
            src_ref=grams.at[sender],
            dst_ref=grams.at[sender],
            send_sem=send_m.at[receiver],
            recv_sem=recv_m.at[sender],
            device_id=(receiver, col),
            device_id_type=MESH,
        )

    peers = [lax.rem(my_row + d, n) for d in range(1, n)]
    for peer in peers:
        gram_copy(my_row, peer).start()
    pl.semaphore_wait(ready, 2)

    pieces = min(8, n) * PARTS
    first = n // 2 * PARTS
    wide = work.shape[1] // 2

    def scatter_step(item, carry):
        way, spot, start = scatter_item(item)
        arrives = spot < last

        @pl.when(item + AHEAD < items)
        def _():
            scatter_counts(item + AHEAD).start()

        scatter_counts(item).wait()

        @pl.when(arrives)
        def _():
            send_sums(way, spot).wait_recv()

        def piece(t, carry):
            here = pl.ds(pl.multiple_of(t * tile, tile), tile)
            product = jnp.dot(left[...], ppmi_at(item, start, t), preferred_element_type=F32)
            product = product[:rank] + product[rank:]

            @pl.when(arrives)
            def _():
                buf[way, spot, :, here] = buf[way, spot, :, here] + product

            @pl.when(jnp.logical_not(arrives))
            def _():
                buf[way, spot, :, here] = product

            return carry

        lax.fori_loop(0, width // tile, piece, 0)

        @pl.when(spot < last + 2 * PARTS)
        def _():
            send_sums(way, spot - 2 * PARTS).start()

        @pl.when(item == first)
        def _():
            for peer in peers:
                gram_copy(peer, my_row).wait_recv()
            gram = grams[0]
            for r in range(1, n):
                gram = gram + grams[r]
            work[...] = jnp.zeros_like(work)
            work[:, :rank] = gram
            shape = (rank, wide)
            same = lax.broadcasted_iota(jnp.int32, shape, 0) == lax.broadcasted_iota(
                jnp.int32, shape, 1
            )
            work[:, wide:] = jnp.where(same, 1.0, 0.0)

        @pl.when(jnp.logical_and(item >= first, item < first + pieces))
        def _():
            steps = rank // pieces

            def turn(k, carry):
                eliminate(work, (item - first) * steps + k)
                return carry

            lax.fori_loop(0, steps, turn, 0)

        return carry

    lax.fori_loop(0, items, scatter_step, 0)
    above = lax.broadcasted_iota(jnp.int32, (rank, wide), 0) <= lax.broadcasted_iota(
        jnp.int32, (rank, wide), 1
    )
    upper_ref[...] = jnp.where(above, work[:, :wide], 0.0)[:, :rank]
    inverse = twice(work[:, wide:])

    def arrived(count, carry):
        for way in range(2):
            send_sums(way, 2 * PARTS - 1 - count).wait_recv()
        return carry

    def finish(count, carry):
        part = PARTS - 1 - count
        for way in range(2):
            send_sums(way, part).wait_recv()
        for half in range(2):
            def piece(t, carry, half=half):
                here = pl.ds(pl.multiple_of(t * tile, tile), tile)
                there = (half * PARTS + part) * width + t * tile
                high, low = split(
                    buf[half, last + 2 * PARTS + part, :, here]
                    + buf[0, half * PARTS + part, :, here]
                    + buf[1, (1 - half) * PARTS + part, :, here]
                )
                gap = jnp.zeros((wide - rank, tile), BF16)
                sums = jnp.concatenate([high, gap, low, gap], axis=0)
                product = jnp.dot(inverse, sums, preferred_element_type=F32)
                out_ref[:, pl.ds(pl.multiple_of(there, tile), tile)] = (
                    product[:rank] + product[rank:]
                )
                return carry

            lax.fori_loop(0, width // tile, piece, 0)
        return carry

    lax.fori_loop(0, PARTS, arrived, 0)
    lax.fori_loop(0, PARTS, finish, 0)

    def sums_sent(spot, carry):
        send_sums(0, spot).wait_send()
        send_sums(1, spot).wait_send()
        return carry

    lax.fori_loop(0, last, sums_sent, 0)
    for other in others:
        image_copy(col, other).wait_send()
    for peer in peers:
        gram_copy(my_row, peer).wait_send()


def per_device(n, m, counts, row_total, col_total, grand_total, sketch):
    rows, columns = counts.shape
    shard, rank = sketch.shape
    width = shard // (2 * PARTS)
    row_log = (jnp.log(grand_total[0]) - jnp.log(row_total))[:, None]
    vmem, anywhere = pl.BlockSpec(memory_space=pltpu.VMEM), pl.BlockSpec(memory_space=pl.ANY)
    dma = pltpu.SemaphoreType.DMA
    padded = (rank + 127) // 128 * 128
    column_factors, upper = pl.pallas_call(
        functools.partial(round_kernel, n, m),
        out_shape=[
            jax.ShapeDtypeStruct((rank, shard), F32),
            jax.ShapeDtypeStruct((rank, rank), F32),
        ],
        in_specs=[anywhere, vmem, vmem, anywhere],
        out_specs=[vmem, vmem],
        scratch_shapes=[
            pltpu.VMEM((2, (n + 2) * PARTS, rank, width), F32),
            pltpu.VMEM((AHEAD + 1, rows, width), jnp.int32),
            pltpu.VMEM((2 * rank, 2 * rows), F32),
            pltpu.VMEM((m, rank, rows), F32),
            pltpu.VMEM((n, rank, rank), F32),
            pltpu.VMEM((2 * rank, 2 * rows), BF16),
            pltpu.VMEM((rank, 2 * padded), F32),
            dma((2, (n - 1) * PARTS)),
            dma((2, (n - 1) * PARTS)),
            dma((2, (n - 1) * PARTS)),
            dma((2, (n - 1) * PARTS)),
            dma((AHEAD + 1,)),
            dma((2, 2 * PARTS)),
            dma((m,)),
            dma((m,)),
            dma((n,)),
            dma((n,)),
            pltpu.SemaphoreType.REGULAR,
        ],
        compiler_params=pltpu.CompilerParams(
            collective_id=0, has_side_effects=True, vmem_limit_bytes=VMEM_BYTES
        ),
        cost_estimate=pl.CostEstimate(
            flops=16 * rows * columns * rank,
            bytes_accessed=8 * rows * columns,
            transcendentals=2 * rows * columns,
        ),
        name="power_round",
    )(counts, row_log, col_total[None, :], sketch.T)
    return (column_factors.T, upper.T)


def solution(mesh):
    return jax.shard_map(
        functools.partial(per_device, mesh.shape["row"], mesh.shape["col"]),
        mesh=mesh,
        in_specs=(P("row", "col"), P("row"), P("col"), P(), P(("col", "row"), None)),
        out_specs=(P(("col", "row"), None), P()),
        check_vma=False,
    )
```

```python
import functools

import jax
import jax.numpy as jnp
from jax import lax
from jax.experimental import pallas as pl
from jax.experimental.pallas import tpu as pltpu
from jax.sharding import PartitionSpec as P

MESH = pl.DeviceIdType.MESH
VMEM_BYTES = 44 * 2**20
PARTS = 4
AHEAD = 3
F32, BF16 = jnp.float32, jnp.bfloat16


def ring_place(row, n):
    odd = lax.rem(row, 2)
    up = lax.div(row, 2)
    return (1 - odd) * up + odd * (n - 1 - up)


def ring_row(place, n):
    back = lax.div(place, n // 2)
    return (1 - back) * 2 * place + back * (2 * (n - 1 - place) + 1)


def neighbours(n):
    me = ring_place(lax.axis_index("row"), n)
    after = ring_row(lax.rem(me + 1, n), n)
    before = ring_row(lax.rem(me + n - 1, n), n)
    return me, after, before


def meet(n, m):
    row, col = lax.axis_index("row"), lax.axis_index("col")
    barrier = pltpu.get_barrier_semaphore()
    for d in range(1, n):
        pl.semaphore_signal(
            barrier, inc=1, device_id=(lax.rem(row + d, n), col), device_id_type=MESH
        )
    for d in range(1, m):
        pl.semaphore_signal(
            barrier, inc=1, device_id=(row, lax.rem(col + d, m)), device_id_type=MESH
        )
    pl.semaphore_wait(barrier, n + m - 2)


def split(x):
    high = x.astype(BF16)
    return high, (x - high.astype(F32)).astype(BF16)


def ppmi_parts(counts, row_log, col_total):
    pmi = jnp.log(jnp.maximum(counts.astype(F32), 1.0)) + row_log - jnp.log(col_total)
    ppmi = jnp.where(counts > 0, jnp.maximum(pmi, 0.0), 0.0)
    return jnp.concatenate(split(ppmi), axis=0)


def tile_width(half):
    width = 1024
    while half % width:
        width //= 2
    return width


def columns_of(place, half, part, width, n):
    start = ring_row(place, n) * (2 * PARTS * width) + (half * PARTS + part) * width
    return pl.multiple_of(start, 128)


def counts_copy(counts_ref, held, sem, item, start, width):
    slot = lax.rem(item, AHEAD + 1)
    return pltpu.make_async_copy(
        counts_ref.at[:, pl.ds(start, width)], held.at[slot], sem.at[slot]
    )


def twice(x):
    high, low = split(x)
    return jnp.concatenate(
        [jnp.concatenate([high, high], axis=1), jnp.concatenate([low, low], axis=1)], axis=0
    )


def eliminate(work, k):
    rank, wide = work.shape
    lanes = lax.broadcasted_iota(jnp.int32, (1, wide // 2), 1)
    rows = lax.broadcasted_iota(jnp.int32, (rank, 1), 0)
    now = work[...]
    row = work[pl.ds(k, 1), :]
    column = jnp.sum(jnp.where(lanes == k, now[:, : wide // 2], 0.0), axis=1, keepdims=True)
    pivot = jnp.sum(jnp.where(lanes == k, row[:, : wide // 2], 0.0), axis=1, keepdims=True)
    root = jnp.sqrt(pivot)
    row = row / root
    rest = now - jnp.where(rows > k, column / root, 0.0) * row
    work[...] = jnp.where(rows == k, row, rest)


def round_kernel(
    n, m, counts_ref, row_log_ref, col_ref, sketch_ref, out_ref, upper_ref,
    buf, held, total, images, grams, left, work,
    send_g, recv_g, send_s, recv_s, counts_sem, own_sem,
    send_i, recv_i, send_m, recv_m, ready,
):
    width = buf.shape[3]
    rank = buf.shape[2]
    rows = row_log_ref.shape[0]
    tile = tile_width(width)
    me, after, before = neighbours(n)
    my_row, col = lax.axis_index("row"), lax.axis_index("col")
    last = (n - 1) * PARTS
    items = 2 * n * PARTS

    def target(way):
        return ((1 - way) * after + way * before, col)

    def gather_item(item):
        extra = lax.max(item - 2 * PARTS, 0)
        far = lax.min(lax.div(item, 2 * PARTS), 1)
        way = far * lax.rem(extra, 2)
        spot = (1 - far) * item + far * (2 * PARTS + lax.div(extra, 2))
        slot, part = lax.div(spot, PARTS), lax.rem(spot, PARTS)
        distance = lax.div(slot, 2)
        odd = lax.rem(slot, 2)
        half = (1 - way) * odd + way * (1 - odd)
        place = lax.rem(me + n + (2 * way - 1) * distance, n)
        return way, spot, columns_of(place, half, part, width, n)

    def scatter_item(item):
        way = lax.rem(item, 2)
        count = lax.div(item, 2)
        own = lax.div(count, last)
        spot = (1 - own) * (last + 2 * PARTS - 1 - count) + own * (2 * PARTS + count)
        slot, part = lax.div(spot, PARTS), lax.rem(spot, PARTS)
        distance = (1 - own) * lax.div(slot, 2)
        odd = lax.rem(slot, 2)
        half = (1 - own) * ((1 - way) * odd + way * (1 - odd)) + own * way
        place = lax.rem(me + n + (1 - 2 * way) * distance, n)
        return way, spot, columns_of(place, half, part, width, n)

    def send_sketch(way, spot):
        return pltpu.make_async_remote_copy(
            src_ref=buf.at[way, spot],
            dst_ref=buf.at[way, spot + 2 * PARTS],
            send_sem=send_g.at[way, spot],
            recv_sem=recv_g.at[way, spot],
            device_id=target(way),
            device_id_type=MESH,
        )

    def send_sums(way, spot):
        return pltpu.make_async_remote_copy(
            src_ref=buf.at[way, spot + 2 * PARTS],
            dst_ref=buf.at[way, spot],
            send_sem=send_s.at[way, spot],
            recv_sem=recv_s.at[way, spot],
            device_id=target(way),
            device_id_type=MESH,
        )

    def gather_counts(item):
        return counts_copy(counts_ref, held, counts_sem, item, gather_item(item)[2], width)

    def scatter_counts(item):
        return counts_copy(counts_ref, held, counts_sem, item, scatter_item(item)[2], width)

    def ppmi_at(item, start, t):
        return ppmi_parts(
            held[lax.rem(item, AHEAD + 1), :, pl.ds(pl.multiple_of(t * tile, tile), tile)],
            row_log_ref[...],
            col_ref[:, pl.ds(pl.multiple_of(start + t * tile, 128), tile)],
        )

    own = [
        pltpu.make_async_copy(
            sketch_ref.at[:, pl.ds(((spot + way * PARTS) % (2 * PARTS)) * width, width)],
            buf.at[way, spot],
            own_sem.at[way, spot],
        )
        for spot in range(2 * PARTS)
        for way in range(2)
    ]
    for copy in own:
        copy.start()
    for item in range(AHEAD):
        gather_counts(item).start()
    meet(n, m)
    for at, copy in enumerate(own):
        copy.wait()
        send_sketch(at % 2, at // 2).start()
    total[...] = jnp.zeros_like(total)

    def gather_step(item, carry):
        way, spot, start = gather_item(item)

        @pl.when(item + AHEAD < items)
        def _():
            gather_counts(item + AHEAD).start()

        @pl.when(item >= 2 * PARTS)
        def _():
            send_sketch(way, spot - 2 * PARTS).wait_recv()

            @pl.when(spot < last)
            def _():
                send_sketch(way, spot).start()

        gather_counts(item).wait()

        def piece(t, carry):
            here = pl.ds(pl.multiple_of(t * tile, tile), tile)
            test = jnp.concatenate(split(buf[way, spot, :, here]), axis=0)
            total[...] += lax.dot_general(
                test, ppmi_at(item, start, t), (((1,), (1,)), ((), ())),
                preferred_element_type=F32,
            )
            return carry

        lax.fori_loop(0, width // tile, piece, 0)
        return carry

    lax.fori_loop(0, items, gather_step, 0)
    for item in range(AHEAD):
        scatter_counts(item).start()

    both = total[:rank, :] + total[rank:, :]
    images[col] = both[:, :rows] + both[:, rows:]

    def image_copy(sender, receiver):
        return pltpu.make_async_remote_copy(
            src_ref=images.at[sender],
            dst_ref=images.at[sender],
            send_sem=send_i.at[receiver],
            recv_sem=recv_i.at[sender],
            device_id=(my_row, receiver),
            device_id_type=MESH,
        )

    others = [lax.rem(col + d, m) for d in range(1, m)]
    for other in others:
        image_copy(col, other).start()

    def sketch_sent(spot, carry):
        send_sketch(0, spot).wait_send()
        send_sketch(1, spot).wait_send()
        return carry

    lax.fori_loop(0, last, sketch_sent, 0)
    for way in range(2):
        pl.semaphore_signal(ready, inc=1, device_id=target(way), device_id_type=MESH)
    for other in others:
        image_copy(other, col).wait_recv()
    image = images[0]
    for c in range(1, m):
        image = image + images[c]
    left[...] = twice(image)

    total[:rank, :rows] = image

    def gram_copy(sender, receiver):
        return pltpu.make_async_remote_copy(
            src_ref=grams.at[sender],
            dst_ref=grams.at[sender],
            send_sem=send_m.at[receiver],
            recv_sem=recv_m.at[sender],
            device_id=(receiver, col),
            device_id_type=MESH,
        )

    peers = [lax.rem(my_row + d, n) for d in range(1, n)]
    pl.semaphore_wait(ready, 2)

    pieces = min(8, n) * PARTS
    first = n // 2 * PARTS
    wide = work.shape[1] // 2

    def scatter_step(item, carry):
        way, spot, start = scatter_item(item)
        arrives = spot < last

        @pl.when(item + AHEAD < items)
        def _():
            scatter_counts(item + AHEAD).start()

        scatter_counts(item).wait()

        @pl.when(arrives)
        def _():
            send_sums(way, spot).wait_recv()

        def piece(t, carry):
            here = pl.ds(pl.multiple_of(t * tile, tile), tile)
            product = jnp.dot(left[...], ppmi_at(item, start, t), preferred_element_type=F32)
            product = product[:rank] + product[rank:]

            @pl.when(arrives)
            def _():
                buf[way, spot, :, here] = buf[way, spot, :, here] + product

            @pl.when(jnp.logical_not(arrives))
            def _():
                buf[way, spot, :, here] = product

            return carry

        lax.fori_loop(0, width // tile, piece, 0)

        @pl.when(spot < last + 2 * PARTS)
        def _():
            send_sums(way, spot - 2 * PARTS).start()

        @pl.when(item == PARTS)
        def _():
            mine = total[:rank, :rows]
            grams[my_row] = lax.dot_general(
                mine, mine, (((1,), (1,)), ((), ())),
                precision=lax.Precision.HIGHEST, preferred_element_type=F32,
            )
            for peer in peers:
                gram_copy(my_row, peer).start()

        @pl.when(item == first)
        def _():
            for peer in peers:
                gram_copy(peer, my_row).wait_recv()
            gram = grams[0]
            for r in range(1, n):
                gram = gram + grams[r]
            work[...] = jnp.zeros_like(work)
            work[:, :rank] = gram
            shape = (rank, wide)
            same = lax.broadcasted_iota(jnp.int32, shape, 0) == lax.broadcasted_iota(
                jnp.int32, shape, 1
            )
            work[:, wide:] = jnp.where(same, 1.0, 0.0)

        @pl.when(jnp.logical_and(item >= first, item < first + pieces))
        def _():
            steps = rank // pieces

            def turn(k, carry):
                eliminate(work, (item - first) * steps + k)
                return carry

            lax.fori_loop(0, steps, turn, 0)

        return carry

    lax.fori_loop(0, items, scatter_step, 0)
    above = lax.broadcasted_iota(jnp.int32, (rank, wide), 0) <= lax.broadcasted_iota(
        jnp.int32, (rank, wide), 1
    )
    upper_ref[...] = jnp.where(above, work[:, :wide], 0.0)[:, :rank]
    inverse = twice(work[:, wide:])

    def arrived(count, carry):
        for way in range(2):
            send_sums(way, 2 * PARTS - 1 - count).wait_recv()
        return carry

    def finish(count, carry):
        part = PARTS - 1 - count
        for way in range(2):
            send_sums(way, part).wait_recv()
        for half in range(2):
            def piece(t, carry, half=half):
                here = pl.ds(pl.multiple_of(t * tile, tile), tile)
                there = (half * PARTS + part) * width + t * tile
                high, low = split(
                    buf[half, last + 2 * PARTS + part, :, here]
                    + buf[0, half * PARTS + part, :, here]
                    + buf[1, (1 - half) * PARTS + part, :, here]
                )
                gap = jnp.zeros((wide - rank, tile), BF16)
                sums = jnp.concatenate([high, gap, low, gap], axis=0)
                product = jnp.dot(inverse, sums, preferred_element_type=F32)
                out_ref[:, pl.ds(pl.multiple_of(there, tile), tile)] = (
                    product[:rank] + product[rank:]
                )
                return carry

            lax.fori_loop(0, width // tile, piece, 0)
        return carry

    lax.fori_loop(0, PARTS, arrived, 0)
    lax.fori_loop(0, PARTS, finish, 0)

    def sums_sent(spot, carry):
        send_sums(0, spot).wait_send()
        send_sums(1, spot).wait_send()
        return carry

    lax.fori_loop(0, last, sums_sent, 0)
    for other in others:
        image_copy(col, other).wait_send()
    for peer in peers:
        gram_copy(my_row, peer).wait_send()


def per_device(n, m, counts, row_total, col_total, grand_total, sketch):
    rows, columns = counts.shape
    shard, rank = sketch.shape
    width = shard // (2 * PARTS)
    row_log = (jnp.log(grand_total[0]) - jnp.log(row_total))[:, None]
    vmem, anywhere = pl.BlockSpec(memory_space=pltpu.VMEM), pl.BlockSpec(memory_space=pl.ANY)
    dma = pltpu.SemaphoreType.DMA
    padded = (rank + 127) // 128 * 128
    column_factors, upper = pl.pallas_call(
        functools.partial(round_kernel, n, m),
        out_shape=[
            jax.ShapeDtypeStruct((rank, shard), F32),
            jax.ShapeDtypeStruct((rank, rank), F32),
        ],
        in_specs=[anywhere, vmem, vmem, anywhere],
        out_specs=[vmem, vmem],
        scratch_shapes=[
            pltpu.VMEM((2, (n + 2) * PARTS, rank, width), F32),
            pltpu.VMEM((AHEAD + 1, rows, width), jnp.int32),
            pltpu.VMEM((2 * rank, 2 * rows), F32),
            pltpu.VMEM((m, rank, rows), F32),
            pltpu.VMEM((n, rank, rank), F32),
            pltpu.VMEM((2 * rank, 2 * rows), BF16),
            pltpu.VMEM((rank, 2 * padded), F32),
            dma((2, (n - 1) * PARTS)),
            dma((2, (n - 1) * PARTS)),
            dma((2, (n - 1) * PARTS)),
            dma((2, (n - 1) * PARTS)),
            dma((AHEAD + 1,)),
            dma((2, 2 * PARTS)),
            dma((m,)),
            dma((m,)),
            dma((n,)),
            dma((n,)),
            pltpu.SemaphoreType.REGULAR,
        ],
        compiler_params=pltpu.CompilerParams(
            collective_id=0, has_side_effects=True, vmem_limit_bytes=VMEM_BYTES
        ),
        cost_estimate=pl.CostEstimate(
            flops=16 * rows * columns * rank,
            bytes_accessed=8 * rows * columns,
            transcendentals=2 * rows * columns,
        ),
        name="power_round",
    )(counts, row_log, col_total[None, :], sketch.T)
    return (column_factors.T, upper.T)


def solution(mesh):
    return jax.shard_map(
        functools.partial(per_device, mesh.shape["row"], mesh.shape["col"]),
        mesh=mesh,
        in_specs=(P("row", "col"), P("row"), P("col"), P(), P(("col", "row"), None)),
        out_specs=(P(("col", "row"), None), P()),
        check_vma=False,
    )
```
